256 devices in a mesh: grp: 8 (over x, core), row: 4 (over z_lo), col: 8 (over y, z_hi).
Axes of the slice: x: 4, y: 4, z: 8 (z_hi: 2, z_lo: 4; z = z_hi * 4 + z_lo), core: 2. Of those that a mesh axis runs over, the one named last changes fastest.
Arguments:
- low_t: float32 [8, 4096, 768], P('grp', ('row', 'col')), may hold values from -8 to 8, as said below
- inv_first: float32 [8, 4096, 4096], P('grp', ('row', 'col')), may hold values from -8 to 8, as said below
- coupling_num: int32 [8, 4096, 4096], P('grp', ('row', 'col')), may hold values from -16 to 16
Outputs:
- solved: float32 [8, 4096, 768], P('grp', ('row', 'col'))
- swapped: float32 [8, 4096, 768], P('grp', ('row', 'col'))
The draws below stay inside these ranges and needn't reach their ends.
Inputs may be any that keep to these rules, and one draw needn't show every extreme that they name: low_t[g, k, i] is zero where k > 3328 + i (rows of a lower-triangular matrix); its entries at k = 3328 + i lie in 0.5 to 2. inv_first[g] is lower triangular with diagonal entries in 0.5 to 2.
All inputs are finite; a program needn't handle non-finite values.
Results may differ from the reference program's by a relative error of at most 0.000071.
Values sent between devices are 32-bit elements; how exact they have to be, the bound alone decides.
No kernel may reach another device: no remote copies, remote signals or barrier semaphores. Data moves between devices by JAX's collectives and lax.ppermute only.
A program may use at most 64 MiB of HBM per device.

```python
import math
import jax
import jax.numpy as jnp
from jax import lax

B = 4096
BAND = 6144
ROWS = 768
MERGES = 8


def draw_low_t(key, part):
    key_off, key_diag = jax.random.split(jax.random.fold_in(key, 11), 2)
    depth = jnp.arange(B)[:, None]
    column = jnp.arange(ROWS)[None, :]
    diagonal_at = B - ROWS + column
    off_part = jnp.clip(jax.random.normal(key_off, (MERGES, B, ROWS), jnp.float32), -4.0, 4.0) * (1.5 / math.sqrt(B))
    diag_part = jnp.exp(jax.random.uniform(key_diag, (MERGES, 1, ROWS), jnp.float32, math.log(0.5), math.log(2.0)))
    return jnp.where(depth == diagonal_at, diag_part, jnp.where(depth < diagonal_at, off_part, 0.0)).astype(jnp.float32)


def draw_inv_first(key, part):
    key_off, key_diag = jax.random.split(jax.random.fold_in(key, 23), 2)
    row_index = jnp.arange(B)[:, None]
    col_index = jnp.arange(B)[None, :]
    off_part = jnp.clip(jax.random.normal(key_off, (MERGES, B, B), jnp.float32), -4.0, 4.0) * (1.5 / math.sqrt(B))
    diag_part = jnp.exp(jax.random.uniform(key_diag, (MERGES, B, 1), jnp.float32, math.log(0.5), math.log(2.0)))
    return jnp.where(row_index == col_index, diag_part, jnp.where(col_index < row_index, off_part, 0.0)).astype(jnp.float32)


def plant(drawn, stream_key, least, high):
    index_at = [jax.random.randint(jax.random.fold_in(stream_key, axis), (), 0, length) for axis, length in enumerate(drawn.shape)]
    widest = drawn.shape.index(max(drawn.shape))
    beside = index_at[:widest] + [(index_at[widest] + 1) % drawn.shape[widest]] + index_at[widest + 1:]
    return drawn.at[tuple(index_at)].set(least).at[tuple(beside)].set(high)


def setup_inputs(seed: int = 0) -> dict:
    key_of = jax.random.split(jax.random.key(seed), 4)
    return {
        "low_t": draw_low_t(jax.random.fold_in(key_of[3], 71), 0),
        "inv_first": draw_inv_first(jax.random.fold_in(key_of[3], 71), 0),
        "coupling_num": plant(jax.random.randint(key_of[2], (MERGES, B, B), -16, 17), jax.random.fold_in(key_of[2], 1), -16, 16).astype(jnp.int32),
    }


HIGHEST = lax.Precision.HIGHEST


def reference(low_t, inv_first, coupling_num):
    row_index = jnp.arange(B, dtype=jnp.int32)[:, None]
    col_index = jnp.arange(B, dtype=jnp.int32)[None, :]
    inside = (B + row_index - col_index) <= BAND

    def merge_one(operands):
        low_part, inv_part, num_part = operands
        coupling = jnp.where(inside, num_part.astype(jnp.float32) / 64.0, jnp.float32(0.0))
        product = jnp.dot(coupling.T, low_part, precision=HIGHEST, preferred_element_type=jnp.float32)
        return -jnp.dot(inv_part.T, product, precision=HIGHEST, preferred_element_type=jnp.float32)

    solved = lax.map(merge_one, (low_t, inv_first, coupling_num))
    swapped = solved.reshape(MERGES // 2, 2, B, ROWS)[:, ::-1].reshape(MERGES, B, ROWS)
    return solved, swapped
```

```python
import jax
import jax.numpy as jnp
from jax import lax
from jax.sharding import Mesh, PartitionSpec as P

B = 4096
BAND = 6144
PREC = lax.Precision.HIGH
PARTS = 2


def dot_lead(first, second):
    return lax.dot_general(
        first, second, (((0,), (0,)), ((), ())), precision=PREC,
        preferred_element_type=jnp.float32,
    )


def ring_y(step):
    return [(i, (i + step) % 4) for i in range(4)]


def ring_z(step):
    flat = lambda z: (z % 4) * 2 + z // 4
    return [(flat(z), flat((z + step) % 8)) for z in range(8)]


def move_y(block, step):
    return lax.ppermute(block, "y", ring_y(step))


def move_z(block, step):
    return lax.ppermute(block, ("zl", "zh"), ring_z(step))


def spread(matrix, y):
    rows = matrix.shape[0]
    blocks = matrix.reshape(rows, 4, 4, 2, 128)

    def of(step):
        picked = lax.dynamic_index_in_dim(blocks, (y + step) % 4, axis=2, keepdims=False)
        return picked.transpose(0, 2, 1, 3).reshape(rows, 1024)

    return jnp.concatenate(
        [of(0), move_y(of(1), 1), move_y(of(3), -1), move_y(of(2), 2)], axis=0
    )


def gather_y(block):
    return jnp.concatenate(
        [block, move_y(block, 1), move_y(block, -1), move_y(block, 2)], axis=0
    )


def reduce_z(spread_cols, lead, z):
    def chunk(step):
        cols = lax.dynamic_slice_in_dim(spread_cols, ((z + step) % 8) * 128, 128, axis=1)
        return dot_lead(cols, lead)

    far = chunk(4)
    up = move_z(far[:64], 1)
    down = move_z(far[64:], -1)
    third = chunk(3)
    up = move_z(jnp.concatenate([third[:64] + up, third[64:]], axis=0), 1)
    third = chunk(5)
    down = move_z(jnp.concatenate([third[:64], third[64:] + down], axis=0), -1)
    for step in (2, 1):
        up = move_z(chunk(step) + up, 1)
        down = move_z(chunk(8 - step) + down, -1)
    return chunk(0) + up + down


def local(low_t, inv_first, coupling_num):
    low, inv, num = low_t[0], inv_first[0], coupling_num[0]
    zl, y, zh = lax.axis_index("zl"), lax.axis_index("y"), lax.axis_index("zh")
    z = zh * 4 + zl
    position = zl * 8 + y * 2 + zh
    global_rows = position * 128 + lax.broadcasted_iota(jnp.int32, (128, B), 0)
    global_cols = lax.broadcasted_iota(jnp.int32, (128, B), 1)
    inside = B + global_rows - global_cols <= BAND
    coupling = jnp.where(inside, num.astype(jnp.float32) / 64.0, jnp.float32(0.0))
    coupling = spread(coupling, y)
    width = low.shape[1] // PARTS
    parts = [low[:, i * width:(i + 1) * width] for i in range(PARTS)]
    products = [reduce_z(coupling, gather_y(part), z) for part in parts]
    inv = spread(inv, y)
    solved = [-reduce_z(inv, gather_y(product), z) for product in products]
    core = [(0, 1), (1, 0)]
    swapped = [lax.ppermute(part, "core", core) for part in solved]
    return (
        jnp.concatenate(solved, axis=1)[None],
        jnp.concatenate(swapped, axis=1)[None],
    )


def solution(mesh):
    fine = Mesh(mesh.devices.reshape(4, 2, 4, 4, 2), ("x", "core", "zl", "y", "zh"))
    placed = P(("x", "core"), ("zl", "y", "zh"), None)
    return jax.shard_map(
        local, mesh=fine, in_specs=(placed,) * 3, out_specs=(placed, placed), check_vma=False,
    )
```

```python
import jax
import jax.numpy as jnp
from jax import lax
from jax.experimental import pallas as pl
from jax.experimental.pallas import tpu as pltpu
from jax.sharding import Mesh, PartitionSpec as P

B = 4096
BAND = 6144
ORDER = (0, 3, 1, 2)
CHAINS = 2
WIDTHS = (384, 384)
INV_ALL_TO_ALL = True


def flat_z(z):
    return (z % 4) * 2 + z // 4


def block_of(y, z):
    return (z % 4) * 8 + y * 2 + z // 4


def move_y(block, step):
    return lax.ppermute(block, "y", [(i, (i + step) % 4) for i in range(4)])


def move_z(block, step):
    return lax.ppermute(
        block, ("zl", "zh"), [(flat_z(z), flat_z((z + step) % 8)) for z in range(8)]
    )


def tie(value, *after):
    return lax.optimization_barrier((value, after))[0]


def dot_lead(first, second):
    return lax.dot_general(
        first, second, (((0,), (0,)), ((), ())), precision=lax.Precision.HIGH,
        preferred_element_type=jnp.float32,
    )


def columns(matrix, first, count):
    def kernel(at, *refs):
        for d in range(count):
            target = refs[4 * count + d]
            for zl in range(4):
                source = refs[4 * d + zl]
                target[:, zl * 128:zl * 128 + 128] = source[:, :128]
                target[:, 512 + zl * 128:640 + zl * 128] = source[:, 128:]

    def source(d, zl):
        return pl.BlockSpec((128, 256), lambda i, at: (0, zl * 4 + (at[0] + d) % 4))

    return pl.pallas_call(
        kernel,
        grid_spec=pltpu.PrefetchScalarGridSpec(
            num_scalar_prefetch=1,
            grid=(1,),
            in_specs=[source(d, zl) for d in range(count) for zl in range(4)],
            out_specs=[pl.BlockSpec((128, 1024), lambda i, at: (0, 0))] * count,
        ),
        out_shape=[jax.ShapeDtypeStruct((128, 1024), matrix.dtype)] * count,
        compiler_params=pltpu.CompilerParams(vmem_limit_bytes=24 * 1024 * 1024),
        name="columns",
    )(first, *[matrix] * (4 * count))


def exchange(by_step):
    return [
        by_step[0], move_y(by_step[1], 1), move_y(by_step[3], -1), move_y(by_step[2], 2)
    ]


def gather_y(block):
    return [block, move_y(block, 1), move_y(block, -1), move_y(block, 2)]


def reduce_z(left, rights, z):
    parts = range(CHAINS)
    whole = [
        lax.psum_scatter(
            dot_lead(left, right), ("zh", "zl"), scatter_dimension=0, tiled=True
        )
        for right in rights[CHAINS:]
    ]

    def chunk(step, p):
        block = lax.dynamic_slice_in_dim(left, ((z + step) % 8) * 128, 128, axis=1)
        return dot_lead(block, rights[p])

    far = [chunk(4, p) for p in parts]
    up = [move_z(far[p][:64], 1) for p in parts]
    down = [move_z(far[p][64:], -1) for p in parts]
    for p in parts:
        third = chunk(3, p)
        up[p] = move_z(jnp.concatenate([third[:64] + up[p], third[64:]], axis=0), 1)
        third = chunk(5, p)
        down[p] = move_z(jnp.concatenate([third[:64], third[64:] + down[p]], axis=0), -1)
    for step in (2, 1):
        for p in parts:
            up[p] = move_z(chunk(step, p) + up[p], 1)
            down[p] = move_z(chunk(8 - step, p) + down[p], -1)
    return [chunk(0, p) + up[p] + down[p] for p in parts] + whole


def local(low_t, inv_first, coupling_num):
    low, inv, num = low_t[0], inv_first[0], coupling_num[0]
    zl, y, zh = lax.axis_index("zl"), lax.axis_index("y"), lax.axis_index("zh")
    z = zh * 4 + zl
    me = y.astype(jnp.int32)[None]
    lows = gather_y(low)
    nums = exchange(columns(num, me, 4))
    if INV_ALL_TO_ALL:
        inv = jnp.stack(columns(inv, jnp.zeros_like(me), 4))
        inv = lax.all_to_all(tie(inv, nums), "y", 0, 0, tiled=True)
    else:
        inv = exchange(tie(columns(inv, me, 4), nums))
    row = lax.broadcasted_iota(jnp.int32, (128, 1024), 0)
    column = lax.broadcasted_iota(jnp.int32, (128, 1024), 1)
    global_cols = block_of(y, column // 128) * 128 + column % 128
    pieces = []
    for d, piece in zip(ORDER, nums):
        inside = B + block_of((y + d) % 4, z) * 128 + row - global_cols <= BAND
        pieces.append(jnp.where(inside, piece.astype(jnp.float32) / 64.0, jnp.float32(0.0)))
    starts = [sum(WIDTHS[:i]) for i in range(len(WIDTHS))]
    low = jnp.concatenate(lows, axis=0)
    coupling, low = lax.optimization_barrier((jnp.concatenate(pieces, axis=0), low))
    products = reduce_z(
        coupling, [low[:, at:at + width] for at, width in zip(starts, WIDTHS)], z
    )
    inv = tie(inv, products[0])
    products = [jnp.concatenate(gather_y(product), axis=0) for product in products]
    if INV_ALL_TO_ALL:
        inv = [lax.dynamic_index_in_dim(inv, (y + d) % 4, 0, keepdims=False) for d in ORDER]
    inv = lax.optimization_barrier(jnp.concatenate(inv, axis=0))
    solved = [-part for part in reduce_z(inv, products, z)]
    core = [(0, 1), (1, 0)]
    swapped = [lax.ppermute(part, "core", core) for part in solved]
    return (
        jnp.concatenate(solved, axis=1)[None],
        jnp.concatenate(swapped, axis=1)[None],
    )


def solution(mesh):
    fine = Mesh(mesh.devices.reshape(4, 2, 4, 4, 2), ("x", "core", "zl", "y", "zh"))
    placed = P(("x", "core"), ("zl", "y", "zh"), None)
    return jax.shard_map(
        local, mesh=fine, in_specs=(placed,) * 3, out_specs=(placed, placed), check_vma=False,
    )
```

```python
import jax
import jax.numpy as jnp
from jax import lax
from jax.experimental import pallas as pl
from jax.experimental.pallas import tpu as pltpu
from jax.sharding import Mesh, PartitionSpec as P

B = 4096
BAND = 6144
ORDER = (0, 3, 1, 2)
CHAINS = 2
WIDTHS = (384, 384)
INV_ALL_TO_ALL = True


def flat_z(z):
    return (z % 4) * 2 + z // 4


def block_of(y, z):
    return (z % 4) * 8 + y * 2 + z // 4


def move_y(block, step):
    return lax.ppermute(block, "y", [(i, (i + step) % 4) for i in range(4)])


def move_z(block, step):
    return lax.ppermute(
        block, ("zl", "zh"), [(flat_z(z), flat_z((z + step) % 8)) for z in range(8)]
    )


def tie(value, *after):
    return lax.optimization_barrier((value, after))[0]


def dot_lead(first, second):
    return lax.dot_general(
        first, second, (((0,), (0,)), ((), ())), precision=lax.Precision.HIGH,
        preferred_element_type=jnp.float32,
    )


def columns(matrix, first, count):
    def kernel(at, *refs):
        for d in range(count):
            target = refs[4 * count + d]
            for zl in range(4):
                source = refs[4 * d + zl]
                target[:, zl * 128:zl * 128 + 128] = source[:, :128]
                target[:, 512 + zl * 128:640 + zl * 128] = source[:, 128:]

    def source(d, zl):
        return pl.BlockSpec((128, 256), lambda i, at: (0, zl * 4 + (at[0] + d) % 4))

    return pl.pallas_call(
        kernel,
        grid_spec=pltpu.PrefetchScalarGridSpec(
            num_scalar_prefetch=1,
            grid=(1,),
            in_specs=[source(d, zl) for d in range(count) for zl in range(4)],
            out_specs=[pl.BlockSpec((128, 1024), lambda i, at: (0, 0))] * count,
        ),
        out_shape=[jax.ShapeDtypeStruct((128, 1024), matrix.dtype)] * count,
        compiler_params=pltpu.CompilerParams(vmem_limit_bytes=24 * 1024 * 1024),
        name="columns",
    )(first, *[matrix] * (4 * count))


def exchange(by_step):
    return [
        by_step[0], move_y(by_step[1], 1), move_y(by_step[3], -1), move_y(by_step[2], 2)
    ]


def gather_y(block):
    return [block, move_y(block, 1), move_y(block, -1), move_y(block, 2)]


def reduce_z(left, rights, z):
    parts = range(CHAINS)
    whole = [
        lax.psum_scatter(
            dot_lead(left, right), ("zh", "zl"), scatter_dimension=0, tiled=True
        )
        for right in rights[CHAINS:]
    ]

    def chunk(step, p):
        block = lax.dynamic_slice_in_dim(left, ((z + step) % 8) * 128, 128, axis=1)
        return dot_lead(block, rights[p])

    far = lax.optimization_barrier([chunk(4, p) for p in parts])
    up = [move_z(far[p][:64], 1) for p in parts]
    down = [move_z(far[p][64:], -1) for p in parts]
    thirds = lax.optimization_barrier([(chunk(3, p), chunk(5, p)) for p in parts])
    last = far[0]
    for p in parts:
        third, got = thirds[p][0], tie(up[p], last)
        last = jnp.concatenate([third[:64] + got, third[64:]], axis=0)
        up[p] = move_z(last, 1)
        third, got = thirds[p][1], tie(down[p], last)
        last = jnp.concatenate([third[:64], third[64:] + got], axis=0)
        down[p] = move_z(last, -1)
    for step in (2, 1):
        for p in parts:
            last = chunk(step, p) + tie(up[p], last)
            up[p] = move_z(last, 1)
            last = chunk(8 - step, p) + tie(down[p], last)
            down[p] = move_z(last, -1)
    done = []
    for p in parts:
        last = chunk(0, p) + tie(up[p], last) + down[p]
        done.append(last)
    return done + whole


def local(low_t, inv_first, coupling_num):
    low, inv, num = low_t[0], inv_first[0], coupling_num[0]
    zl, y, zh = lax.axis_index("zl"), lax.axis_index("y"), lax.axis_index("zh")
    z = zh * 4 + zl
    me = y.astype(jnp.int32)[None]
    lows = gather_y(low)
    nums = exchange(columns(num, me, 4))
    if INV_ALL_TO_ALL:
        inv = jnp.stack(columns(inv, jnp.zeros_like(me), 4))
        inv = lax.all_to_all(tie(inv, nums), "y", 0, 0, tiled=True)
    else:
        inv = exchange(tie(columns(inv, me, 4), nums))
    row = lax.broadcasted_iota(jnp.int32, (128, 1024), 0)
    column = lax.broadcasted_iota(jnp.int32, (128, 1024), 1)
    global_cols = block_of(y, column // 128) * 128 + column % 128
    pieces = []
    for d, piece in zip(ORDER, nums):
        inside = B + block_of((y + d) % 4, z) * 128 + row - global_cols <= BAND
        pieces.append(jnp.where(inside, piece.astype(jnp.float32) / 64.0, jnp.float32(0.0)))
    starts = [sum(WIDTHS[:i]) for i in range(len(WIDTHS))]
    low = jnp.concatenate(lows, axis=0)
    coupling, low = lax.optimization_barrier((jnp.concatenate(pieces, axis=0), low))
    products = reduce_z(
        coupling, [low[:, at:at + width] for at, width in zip(starts, WIDTHS)], z
    )
    inv = tie(inv, products[0])
    products = [
        lax.optimization_barrier(jnp.concatenate(gather_y(product), axis=0))
        for product in products
    ]
    if INV_ALL_TO_ALL:
        inv = [lax.dynamic_index_in_dim(inv, (y + d) % 4, 0, keepdims=False) for d in ORDER]
    inv = lax.optimization_barrier(jnp.concatenate(inv, axis=0))
    solved = [-part for part in reduce_z(inv, products, z)]
    core = [(0, 1), (1, 0)]
    swapped = [lax.ppermute(part, "core", core) for part in solved]
    return (
        jnp.concatenate(solved, axis=1)[None],
        jnp.concatenate(swapped, axis=1)[None],
    )


def solution(mesh):
    fine = Mesh(mesh.devices.reshape(4, 2, 4, 4, 2), ("x", "core", "zl", "y", "zh"))
    placed = P(("x", "core"), ("zl", "y", "zh"), None)
    return jax.shard_map(
        local, mesh=fine, in_specs=(placed,) * 3, out_specs=(placed, placed), check_vma=False,
    )
```

```python
import jax
import jax.numpy as jnp
from jax import lax
from jax.experimental import pallas as pl
from jax.experimental.pallas import tpu as pltpu
from jax.sharding import Mesh, PartitionSpec as P

B = 4096
BAND = 6144
ORDER = (0, 3, 1, 2)
CHAINS = 2
WIDTHS = (384, 384)
INV_ALL_TO_ALL = True


def flat_z(z):
    return (z % 4) * 2 + z // 4


def block_of(y, z):
    return (z % 4) * 8 + y * 2 + z // 4


def move_y(block, step):
    return lax.ppermute(block, "y", [(i, (i + step) % 4) for i in range(4)])


def move_z(block, step):
    return lax.ppermute(
        block, ("zl", "zh"), [(flat_z(z), flat_z((z + step) % 8)) for z in range(8)]
    )


def tie(value, *after):
    return lax.optimization_barrier((value, after))[0]


def dot_lead(first, second):
    return lax.dot_general(
        first, second, (((0,), (0,)), ((), ())), precision=lax.Precision.HIGH,
        preferred_element_type=jnp.float32,
    )


def columns(matrix, first, count):
    def kernel(at, *refs):
        for d in range(count):
            target = refs[4 * count + d]
            for zl in range(4):
                source = refs[4 * d + zl]
                target[:, zl * 128:zl * 128 + 128] = source[:, :128]
                target[:, 512 + zl * 128:640 + zl * 128] = source[:, 128:]

    def source(d, zl):
        return pl.BlockSpec((128, 256), lambda i, at: (0, zl * 4 + (at[0] + d) % 4))

    return pl.pallas_call(
        kernel,
        grid_spec=pltpu.PrefetchScalarGridSpec(
            num_scalar_prefetch=1,
            grid=(1,),
            in_specs=[source(d, zl) for d in range(count) for zl in range(4)],
            out_specs=[pl.BlockSpec((128, 1024), lambda i, at: (0, 0))] * count,
        ),
        out_shape=[jax.ShapeDtypeStruct((128, 1024), matrix.dtype)] * count,
        compiler_params=pltpu.CompilerParams(vmem_limit_bytes=24 * 1024 * 1024),
        name="columns",
    )(first, *[matrix] * (4 * count))


def exchange(by_step):
    return [
        by_step[0], move_y(by_step[1], 1), move_y(by_step[3], -1), move_y(by_step[2], 2)
    ]


def gather_y(block):
    return [block, move_y(block, 1), move_y(block, -1), move_y(block, 2)]


def reduce_z(left, rights, z):
    parts = range(CHAINS)
    whole = [
        lax.psum_scatter(
            dot_lead(left, right), ("zh", "zl"), scatter_dimension=0, tiled=True
        )
        for right in rights[CHAINS:]
    ]

    def chunk(step, p):
        block = lax.dynamic_slice_in_dim(left, ((z + step) % 8) * 128, 128, axis=1)
        return dot_lead(block, rights[p])

    far = lax.optimization_barrier([chunk(4, p) for p in parts])
    up = [move_z(far[p][:64], 1) for p in parts]
    down = [move_z(far[p][64:], -1) for p in parts]
    thirds = lax.optimization_barrier([(chunk(3, p), chunk(5, p)) for p in parts])
    last = far[0]
    for p in parts:
        third, got = thirds[p][0], tie(up[p], last)
        last = jnp.concatenate([third[:64] + got, third[64:]], axis=0)
        up[p] = move_z(last, 1)
        third, got = thirds[p][1], tie(down[p], last)
        last = jnp.concatenate([third[:64], third[64:] + got], axis=0)
        down[p] = move_z(last, -1)
    for step in (2, 1):
        for p in parts:
            last = chunk(step, p) + tie(up[p], last)
            up[p] = move_z(last, 1)
            last = chunk(8 - step, p) + tie(down[p], last)
            down[p] = move_z(last, -1)
    done = []
    for p in parts:
        last = chunk(0, p) + tie(up[p], last) + down[p]
        done.append(last)
    return done + whole


def local(low_t, inv_first, coupling_num):
    low, inv, num = low_t[0], inv_first[0], coupling_num[0]
    zl, y, zh = lax.axis_index("zl"), lax.axis_index("y"), lax.axis_index("zh")
    z = zh * 4 + zl
    me = y.astype(jnp.int32)[None]
    before, after = move_y(low, 1), move_y(low, -1)
    nums = columns(num, me, 4)
    nums = [
        nums[0], move_y(nums[1], 1), move_y(nums[3], -1),
        move_y(tie(nums[2], before, after), 2),
    ]
    across = [move_y(before[:64], 1), move_y(after[64:], -1)]
    lows = [low, before, after, *across]
    if INV_ALL_TO_ALL:
        inv = jnp.stack(columns(inv, jnp.zeros_like(me), 4))
        inv = lax.all_to_all(tie(inv, nums), "y", 0, 0, tiled=True)
    else:
        inv = exchange(tie(columns(inv, me, 4), nums))
    row = lax.broadcasted_iota(jnp.int32, (128, 1024), 0)
    column = lax.broadcasted_iota(jnp.int32, (128, 1024), 1)
    global_cols = block_of(y, column // 128) * 128 + column % 128
    pieces = []
    for d, piece in zip(ORDER, nums):
        inside = B + block_of((y + d) % 4, z) * 128 + row - global_cols <= BAND
        pieces.append(jnp.where(inside, piece.astype(jnp.float32) / 64.0, jnp.float32(0.0)))
    starts = [sum(WIDTHS[:i]) for i in range(len(WIDTHS))]
    low = jnp.concatenate(lows, axis=0)
    coupling, low = lax.optimization_barrier((jnp.concatenate(pieces, axis=0), low))
    products = reduce_z(
        coupling, [low[:, at:at + width] for at, width in zip(starts, WIDTHS)], z
    )
    inv = tie(inv, products[0])
    products = [
        lax.optimization_barrier(jnp.concatenate(gather_y(product), axis=0))
        for product in products
    ]
    if INV_ALL_TO_ALL:
        inv = [lax.dynamic_index_in_dim(inv, (y + d) % 4, 0, keepdims=False) for d in ORDER]
    inv = lax.optimization_barrier(jnp.concatenate(inv, axis=0))
    solved = [-part for part in reduce_z(inv, products, z)]
    core = [(0, 1), (1, 0)]
    swapped = [lax.ppermute(part, "core", core) for part in solved]
    return (
        jnp.concatenate(solved, axis=1)[None],
        jnp.concatenate(swapped, axis=1)[None],
    )


def solution(mesh):
    fine = Mesh(mesh.devices.reshape(4, 2, 4, 4, 2), ("x", "core", "zl", "y", "zh"))
    placed = P(("x", "core"), ("zl", "y", "zh"), None)
    return jax.shard_map(
        local, mesh=fine, in_specs=(placed,) * 3, out_specs=(placed, placed), check_vma=False,
    )
```

```python
import jax
import jax.numpy as jnp
from jax import lax
from jax.experimental import pallas as pl
from jax.experimental.pallas import tpu as pltpu
from jax.sharding import Mesh, PartitionSpec as P

B = 4096
BAND = 6144
ORDER = (0, 3, 1, 2)
CHAINS = 2
WIDTHS = (384, 384)
INV_ALL_TO_ALL = True


def flat_z(z):
    return (z % 4) * 2 + z // 4


def block_of(y, z):
    return (z % 4) * 8 + y * 2 + z // 4


def move_y(block, step):
    return lax.ppermute(block, "y", [(i, (i + step) % 4) for i in range(4)])


def move_z(block, step):
    return lax.ppermute(
        block, ("zl", "zh"), [(flat_z(z), flat_z((z + step) % 8)) for z in range(8)]
    )


def tie(value, *after):
    return lax.optimization_barrier((value, after))[0]


def dot_lead(first, second):
    return lax.dot_general(
        first, second, (((0,), (0,)), ((), ())), precision=lax.Precision.HIGH,
        preferred_element_type=jnp.float32,
    )


def columns(matrix, first, count):
    def kernel(at, *refs):
        for d in range(count):
            target = refs[4 * count + d]
            for zl in range(4):
                source = refs[4 * d + zl]
                target[:, zl * 128:zl * 128 + 128] = source[:, :128]
                target[:, 512 + zl * 128:640 + zl * 128] = source[:, 128:]

    def source(d, zl):
        return pl.BlockSpec((128, 256), lambda i, at: (0, zl * 4 + (at[0] + d) % 4))

    return pl.pallas_call(
        kernel,
        grid_spec=pltpu.PrefetchScalarGridSpec(
            num_scalar_prefetch=1,
            grid=(1,),
            in_specs=[source(d, zl) for d in range(count) for zl in range(4)],
            out_specs=[pl.BlockSpec((128, 1024), lambda i, at: (0, 0))] * count,
        ),
        out_shape=[jax.ShapeDtypeStruct((128, 1024), matrix.dtype)] * count,
        compiler_params=pltpu.CompilerParams(vmem_limit_bytes=24 * 1024 * 1024),
        name="columns",
    )(first, *[matrix] * (4 * count))


def exchange(by_step):
    return [
        by_step[0], move_y(by_step[1], 1), move_y(by_step[3], -1), move_y(by_step[2], 2)
    ]


def gather_y(block):
    before, after = move_y(block, 1), move_y(block, -1)
    return [block, before, after, move_y(before[:64], 1), move_y(after[64:], -1)]


def reduce_z(left, rights, z):
    parts = range(CHAINS)
    whole = [
        lax.psum_scatter(
            dot_lead(left, right), ("zh", "zl"), scatter_dimension=0, tiled=True
        )
        for right in rights[CHAINS:]
    ]

    def chunk(step, p):
        block = lax.dynamic_slice_in_dim(left, ((z + step) % 8) * 128, 128, axis=1)
        return dot_lead(block, rights[p])

    far = lax.optimization_barrier([chunk(4, p) for p in parts])
    up = [move_z(far[p][:64], 1) for p in parts]
    down = [move_z(far[p][64:], -1) for p in parts]
    thirds = lax.optimization_barrier([(chunk(3, p), chunk(5, p)) for p in parts])
    last = far[0]
    for p in parts:
        third, got = thirds[p][0], tie(up[p], last)
        last = jnp.concatenate([third[:64] + got, third[64:]], axis=0)
        up[p] = move_z(last, 1)
        third, got = thirds[p][1], tie(down[p], last)
        last = jnp.concatenate([third[:64], third[64:] + got], axis=0)
        down[p] = move_z(last, -1)
    for step in (2, 1):
        for p in parts:
            last = chunk(step, p) + tie(up[p], last)
            up[p] = move_z(last, 1)
            last = chunk(8 - step, p) + tie(down[p], last)
            down[p] = move_z(last, -1)
    done = []
    for p in parts:
        last = chunk(0, p) + tie(up[p], last) + down[p]
        done.append(last)
    return done + whole


def local(low_t, inv_first, coupling_num):
    low, inv, num = low_t[0], inv_first[0], coupling_num[0]
    zl, y, zh = lax.axis_index("zl"), lax.axis_index("y"), lax.axis_index("zh")
    z = zh * 4 + zl
    me = y.astype(jnp.int32)[None]
    before, after = move_y(low, 1), move_y(low, -1)
    nums = columns(num, me, 4)
    nums = [
        nums[0], move_y(nums[1], 1), move_y(nums[3], -1),
        move_y(tie(nums[2], before, after), 2),
    ]
    across = [move_y(before[:64], 1), move_y(after[64:], -1)]
    lows = [low, before, after, *across]
    if INV_ALL_TO_ALL:
        inv = jnp.stack(columns(inv, jnp.zeros_like(me), 4))
        inv = lax.all_to_all(tie(inv, nums), "y", 0, 0, tiled=True)
    else:
        inv = exchange(tie(columns(inv, me, 4), nums))
    row = lax.broadcasted_iota(jnp.int32, (128, 1024), 0)
    column = lax.broadcasted_iota(jnp.int32, (128, 1024), 1)
    global_cols = block_of(y, column // 128) * 128 + column % 128
    pieces = []
    for d, piece in zip(ORDER, nums):
        inside = B + block_of((y + d) % 4, z) * 128 + row - global_cols <= BAND
        pieces.append(jnp.where(inside, piece.astype(jnp.float32) / 64.0, jnp.float32(0.0)))
    starts = [sum(WIDTHS[:i]) for i in range(len(WIDTHS))]
    low = jnp.concatenate(lows, axis=0)
    coupling, low = lax.optimization_barrier((jnp.concatenate(pieces, axis=0), low))
    products = reduce_z(
        coupling, [low[:, at:at + width] for at, width in zip(starts, WIDTHS)], z
    )
    inv = tie(inv, products[0])
    products = [
        lax.optimization_barrier(jnp.concatenate(gather_y(product), axis=0))
        for product in products
    ]
    if INV_ALL_TO_ALL:
        inv = [lax.dynamic_index_in_dim(inv, (y + d) % 4, 0, keepdims=False) for d in ORDER]
    inv = lax.optimization_barrier(jnp.concatenate(inv, axis=0))
    solved = [-part for part in reduce_z(inv, products, z)]
    core = [(0, 1), (1, 0)]
    swapped = [lax.ppermute(part, "core", core) for part in solved]
    return (
        jnp.concatenate(solved, axis=1)[None],
        jnp.concatenate(swapped, axis=1)[None],
    )


def solution(mesh):
    fine = Mesh(mesh.devices.reshape(4, 2, 4, 4, 2), ("x", "core", "zl", "y", "zh"))
    placed = P(("x", "core"), ("zl", "y", "zh"), None)
    return jax.shard_map(
        local, mesh=fine, in_specs=(placed,) * 3, out_specs=(placed, placed), check_vma=False,
    )
```
